32 devices in a mesh: dp: 16 (over z, y, x), cls: 2 (over core).
Axes of the slice: x: 2, y: 2, z: 4, core: 2. Of those that a mesh axis runs over, the one named last changes fastest.
Arguments:
- scores: bfloat16 [32768, 1024], P('dp', 'cls'), may hold values from -4 to 250
- labels: int32 [32768], P('dp'), may hold values from 0 to 1023
- node_ids: int32 [32768], P('dp'), may hold values from 0 to 3
- codes: int32 [32768, 512], P('dp', 'cls'), may hold values from 0 to 255
- sketch: float32 [1024, 8], P('cls'), may hold values from -4 to 4
Outputs:
- histogram: float32 [256, 4, 9, 512], P('dp', None, None, 'cls')
The draws below stay inside these ranges and needn't reach their ends.
All inputs are finite; a program needn't handle non-finite values.
Results may differ from the reference program's by a relative error of at most 0.002.
Values may be sent and summed in bfloat16 or wider, within the bound.
A program may use at most 128 MiB of HBM per device.

```python
import math
import jax
import jax.numpy as jnp
from jax import lax

C = 1024
F = 512
BINS = 256
K = 8
NODES = 4
STATS = 9
ROWS = 32768


def draw_scores(key, part):
    key = jax.random.fold_in(key, 11)
    keys = jax.random.split(key, 1)
    values = jnp.clip(1.5 * jax.random.normal(keys[0], (ROWS, C), jnp.float32), -4.0, 4.0)
    return values.astype(jnp.bfloat16)


def set_ends(values, key, low, high):
    dims = values.shape
    spot = [jax.random.randint(jax.random.fold_in(key, axis), (), 0, dims[axis]) for axis in range(len(dims))]
    values = values.at[tuple(spot)].set(low)
    longest = dims.index(max(dims))
    spot[longest] = (spot[longest] + 1) % dims[longest]
    return values.at[tuple(spot)].set(high)


def block_levels(stream_key, extent, cuts, smallest, high):
    def one(position, blocks):
        heights = jax.random.uniform(jax.random.fold_in(jax.random.fold_in(stream_key, 6), position), (blocks,), jnp.float32, smallest / len(cuts), high / len(cuts))
        return jnp.repeat(jnp.exp(heights), extent[position] // blocks).reshape((-1,) + (1,) * (len(extent) - position - 1))

    gain = one(*cuts[0])
    for cut in cuts[1:]:
        gain = gain * one(*cut)
    return gain


def scatter_about(stream_key, dims, spread, most, shards=(), held_as=jnp.bfloat16):
    factor_of = block_levels(stream_key, dims, shards, -0.22, 0.18) if shards else 1.0
    entries = jax.random.normal(stream_key, dims, jnp.float32) * spread * factor_of
    return jnp.minimum(jnp.maximum(entries, -most), most).astype(held_as)


def setup_inputs(seed: int = 0) -> dict:
    splits = jax.random.split(jax.random.key(seed), 6)
    scores = draw_scores(jax.random.fold_in(splits[5], 71), 0)
    labels = set_ends(jax.random.randint(splits[1], (ROWS,), 0, C), jax.random.fold_in(splits[1], 1), 0, C - 1).astype(jnp.int32)
    node_ids = set_ends(jax.random.randint(splits[2], (ROWS,), 0, NODES), jax.random.fold_in(splits[2], 1), 0, NODES - 1).astype(jnp.int32)
    codes = set_ends(jax.random.randint(splits[3], (ROWS, F), 0, BINS), jax.random.fold_in(splits[3], 1), 0, BINS - 1).astype(jnp.int32)
    sketch = scatter_about(splits[4], (C, K), 1.0, 4.0, ((0, 2),), jnp.float32)
    return {"scores": scores, "labels": labels, "node_ids": node_ids, "codes": codes, "sketch": sketch}


def row_block(score_block, label_block, sketch):
    values = score_block.astype(jnp.float32)
    top = jnp.max(values, axis=1, keepdims=True)
    expo = jnp.exp(values - top)
    probs = expo / jnp.sum(expo, axis=1, keepdims=True)
    grad = jnp.dot(probs, sketch, precision=lax.Precision.HIGHEST) - sketch[label_block]
    hessian = 1.0 - jnp.sum(probs * probs, axis=1, keepdims=True)
    return jnp.concatenate([grad, hessian], axis=1)


def reference(scores, labels, node_ids, codes, sketch):
    block = math.gcd(ROWS, 8192)
    stats = lax.map(lambda pair: row_block(pair[0], pair[1], sketch),
                    (scores.reshape(ROWS // block, block, C), labels.reshape(ROWS // block, block)))
    stats = stats.reshape(ROWS, STATS)
    member = (node_ids[:, None] == jnp.arange(NODES, dtype=jnp.int32)[None, :]).astype(jnp.float32)
    weighted = (member[:, :, None] * stats[:, None, :]).reshape(ROWS, NODES * STATS).astype(jnp.bfloat16)
    weighted = lax.optimization_barrier(weighted).astype(jnp.float32)

    def per_feature(column):
        return jax.ops.segment_sum(weighted, column, num_segments=BINS)

    hist = lax.map(per_feature, codes.T)
    return hist.reshape(F, BINS, NODES, STATS).transpose(1, 2, 3, 0)
```

```python
import functools

import jax
import jax.numpy as jnp
from jax import lax
from jax.experimental import pallas as pl
from jax.experimental.pallas import tpu as pltpu
from jax.sharding import PartitionSpec as P

BINS = 256
NODES = 4
STATS = 9
SLOT = 16
HIGH = lax.Precision.HIGHEST
NT = (((1,), (1,)), ((), ()))


def codes_kernel(codes_ref, out_ref):
    out_ref[...] = codes_ref[...].astype(jnp.float32).T.astype(jnp.bfloat16)


def softmax_kernel(scores_ref, labels_ref, sketch_ref, out_ref):
    values = scores_ref[...].astype(jnp.float32)
    rows, classes = values.shape
    top = jnp.max(values, axis=1, keepdims=True)
    expo = jnp.exp(values - top)
    left = sketch_ref[...]
    sums = lax.dot_general(left, expo, NT, precision=HIGH, preferred_element_type=jnp.float32)
    squares = lax.dot_general(
        left[8:16], expo * expo, NT, precision=HIGH, preferred_element_type=jnp.float32
    )
    hit = lax.broadcasted_iota(jnp.int32, (classes, rows), 0) == labels_ref[...]
    picked = jnp.dot(
        left[0:8], hit.astype(jnp.float32), precision=HIGH, preferred_element_type=jnp.float32
    )
    tops = jnp.broadcast_to(top, (rows, 128)).T[0:1]
    out_ref[0:8] = sums[0:8]
    out_ref[8:16] = picked
    where = lax.broadcasted_iota(jnp.int32, (8, rows), 0)
    out_ref[16:24] = jnp.where(where == 0, tops, jnp.where(where == 1, sums[8:9], squares[0:1]))


def stats_kernel(parts_ref, nodes_ref, out_ref):
    parts = parts_ref.shape[0]
    top = parts_ref[0, 16:17]
    for i in range(1, parts):
        top = jnp.maximum(top, parts_ref[i, 16:17])
    sketched = label = total = squares = 0.0
    for i in range(parts):
        scale = jnp.exp(parts_ref[i, 16:17] - top)
        sketched += parts_ref[i, 0:8] * scale
        label += parts_ref[i, 8:16]
        total += parts_ref[i, 17:18] * scale
        squares += parts_ref[i, 18:19] * (scale * scale)
    grad = sketched / total - label
    hessian = 1.0 - squares / (total * total)
    where = lax.broadcasted_iota(jnp.int32, grad.shape, 0)
    tail = jnp.where(where == 0, hessian, jnp.where(where == 1, nodes_ref[...].astype(jnp.float32), 0.0))
    out_ref[...] = jnp.concatenate([grad, tail], axis=0).astype(jnp.bfloat16)


def hist_kernel(pair, width, codes_ref, stats_ref, out_ref, left_ref, acc_ref):
    step = pl.program_id(0)
    rows = stats_ref.shape[2]
    feats = codes_ref.shape[1]
    groups = feats // pair

    @pl.when(step == 0)
    def _():
        acc_ref[...] = jnp.zeros_like(acc_ref)

    stats = stats_ref[0]
    node = stats[STATS:STATS + 1].astype(jnp.float32)
    wide = stats.astype(jnp.float32)
    wide = jnp.where(lax.broadcasted_iota(jnp.int32, wide.shape, 0) < STATS, wide, 0.0)
    blank = jnp.zeros((NODES * SLOT, rows), jnp.bfloat16)
    member = jnp.concatenate(
        [jnp.where(node == n, wide, 0.0).astype(jnp.bfloat16) for n in range(NODES)], axis=0
    )
    for i in range(pair):
        left_ref[i] = jnp.concatenate([member if i == k else blank for k in range(2)], axis=0)

    bins = lax.broadcasted_iota(jnp.int32, (BINS, width), 0).astype(jnp.bfloat16)
    one = jnp.ones((), jnp.bfloat16)
    zero = jnp.zeros((), jnp.bfloat16)
    for g in range(groups):
        total = acc_ref[g]
        for i in range(pair):
            for c in range(rows // width):
                cut = slice(c * width, (c + 1) * width)
                row = i * groups + g
                code = codes_ref[0, row:row + 1, cut]
                hit = jnp.where(code == bins, one, zero)
                total += lax.dot_general(
                    hit, left_ref[i, :, cut], NT, preferred_element_type=jnp.float32
                )
        acc_ref[g] = total

    @pl.when(step == pl.num_programs(0) - 1)
    def _():
        for g in range(groups):
            out_ref[:, g, :] = acc_ref[g]


def place_kernel(pair, in_ref, out_ref):
    devices, _, groups, lanes = in_ref.shape
    span = devices * groups
    block = in_ref[:, 0].reshape(span, lanes).T
    for i in range(pair):
        for n in range(NODES):
            at = (i * NODES + n) * SLOT
            out_ref[0, n, :, i * span:(i + 1) * span] = block[at:at + STATS]


def body(dp, scores, labels, node_ids, codes, sketch):
    rows, classes = scores.shape
    feats = codes.shape[1]
    own = feats // dp
    pair = 2 if own % 2 == 0 else 1
    groups = own // pair
    block = min(512, rows)

    codes_t = pl.pallas_call(
        codes_kernel,
        grid=(rows // block,),
        in_specs=[pl.BlockSpec((block, feats), lambda i: (i, 0))],
        out_specs=pl.BlockSpec((feats, block), lambda i: (0, i)),
        out_shape=jax.ShapeDtypeStruct((feats, rows), jnp.bfloat16),
    )(codes)
    codes_t = codes_t.reshape(pair, dp, groups, rows).transpose(1, 0, 2, 3).reshape(dp, own, rows)
    codes_all = lax.all_to_all(codes_t, "dp", 0, 0, tiled=True)

    local = (labels - lax.axis_index("cls") * classes)[None, :]
    left = jnp.concatenate(
        [sketch.T, jnp.ones((1, classes), jnp.float32), jnp.zeros((7, classes), jnp.float32)], axis=0
    )
    parts = pl.pallas_call(
        softmax_kernel,
        grid=(rows // block,),
        in_specs=[
            pl.BlockSpec((block, classes), lambda i: (i, 0)),
            pl.BlockSpec((1, block), lambda i: (0, i)),
            pl.BlockSpec((16, classes), lambda i: (0, 0)),
        ],
        out_specs=pl.BlockSpec((24, block), lambda i: (0, i)),
        out_shape=jax.ShapeDtypeStruct((24, rows), jnp.float32),
    )(scores, local, left)
    parts = lax.all_gather(parts, "cls")
    stats = pl.pallas_call(
        stats_kernel,
        out_shape=jax.ShapeDtypeStruct((SLOT, rows), jnp.bfloat16),
    )(parts, node_ids[None, :])
    stats = lax.all_gather(stats, "dp")

    hist = pl.pallas_call(
        functools.partial(hist_kernel, pair, min(WIDTH, rows)),
        grid=(dp,),
        in_specs=[
            pl.BlockSpec((1, own, rows), lambda i: (i, 0, 0)),
            pl.BlockSpec((1, SLOT, rows), lambda i: (i, 0, 0)),
        ],
        out_specs=pl.BlockSpec((BINS, groups, 128), lambda i: (0, 0, 0)),
        out_shape=jax.ShapeDtypeStruct((BINS, groups, 128), jnp.float32),
        scratch_shapes=[
            pltpu.VMEM((pair, 128, rows), jnp.bfloat16),
            pltpu.VMEM((groups, BINS, 128), jnp.float32),
        ],
        compiler_params=pltpu.CompilerParams(vmem_limit_bytes=40 << 20),
    )(codes_all, stats)
    bins = BINS // dp
    hist = lax.all_to_all(hist.reshape(dp, bins, groups, 128), "dp", 0, 0, tiled=True)
    return pl.pallas_call(
        functools.partial(place_kernel, pair),
        grid=(bins,),
        in_specs=[pl.BlockSpec((dp, 1, groups, 128), lambda i: (0, i, 0, 0))],
        out_specs=pl.BlockSpec((1, NODES, STATS, feats), lambda i: (i, 0, 0, 0)),
        out_shape=jax.ShapeDtypeStruct((bins, NODES, STATS, feats), jnp.float32),
    )(hist)


WIDTH = 256


def solution(mesh):
    return jax.shard_map(
        functools.partial(body, mesh.shape["dp"]),
        mesh=mesh,
        in_specs=(P("dp", "cls"), P("dp"), P("dp"), P("dp", "cls"), P("cls", None)),
        out_specs=P("dp", None, None, "cls"),
        check_vma=False,
    )
```

```python
import functools

import jax
import jax.numpy as jnp
from jax import lax
from jax.experimental import pallas as pl
from jax.experimental.pallas import tpu as pltpu
from jax.sharding import PartitionSpec as P

BINS = 256
NODES = 4
STATS = 9
SLOT = 16
HIGH = lax.Precision.HIGHEST
MESH = pl.DeviceIdType.MESH
F8 = jnp.float8_e4m3fn
FIRST, SECOND, THIRD = 32.0, 16.0, float(2**22)
NT = (((1,), (1,)), ((), ()))


def codes_kernel(codes_ref, out_ref):
    out_ref[...] = codes_ref[...].astype(jnp.float32).T.astype(jnp.bfloat16)


def softmax_kernel(scores_ref, labels_ref, sketch_ref, out_ref):
    values = scores_ref[...].astype(jnp.float32)
    rows, classes = values.shape
    top = jnp.max(values, axis=1, keepdims=True)
    expo = jnp.exp(values - top)
    left = sketch_ref[...]
    sums = lax.dot_general(left, expo, NT, precision=HIGH, preferred_element_type=jnp.float32)
    squares = lax.dot_general(
        left[8:16], expo * expo, NT, precision=HIGH, preferred_element_type=jnp.float32
    )
    hit = lax.broadcasted_iota(jnp.int32, (classes, rows), 0) == labels_ref[...]
    picked = jnp.dot(
        left[0:8], hit.astype(jnp.float32), precision=HIGH, preferred_element_type=jnp.float32
    )
    tops = jnp.broadcast_to(top, (rows, 128)).T[0:1]
    out_ref[0:8] = sums[0:8]
    out_ref[8:16] = picked
    where = lax.broadcasted_iota(jnp.int32, (8, rows), 0)
    out_ref[16:24] = jnp.where(where == 0, tops, jnp.where(where == 1, sums[8:9], squares[0:1]))


def combine(parts_ref, nodes_ref):
    parts = parts_ref.shape[0]
    top = parts_ref[0, 16:17]
    for i in range(1, parts):
        top = jnp.maximum(top, parts_ref[i, 16:17])
    sketched = label = total = squares = 0.0
    for i in range(parts):
        scale = jnp.exp(parts_ref[i, 16:17] - top)
        sketched += parts_ref[i, 0:8] * scale
        label += parts_ref[i, 8:16]
        total += parts_ref[i, 17:18] * scale
        squares += parts_ref[i, 18:19] * (scale * scale)
    grad = sketched / total - label
    hessian = 1.0 - squares / (total * total)
    where = lax.broadcasted_iota(jnp.int32, grad.shape, 0)
    tail = jnp.where(where == 0, hessian, jnp.where(where == 1, nodes_ref[...].astype(jnp.float32), 0.0))
    return jnp.concatenate([grad, tail], axis=0).astype(jnp.bfloat16)


def split_weights(stats, left_ref):
    node = stats[STATS:STATS + 1]
    wide = stats.astype(jnp.float32) * FIRST
    wide = jnp.where(lax.broadcasted_iota(jnp.int32, wide.shape, 0) < STATS, wide, 0.0)
    first = wide.astype(F8).astype(jnp.float32)
    rest = wide - first
    second = (rest * SECOND).astype(F8).astype(jnp.float32)
    third = ((rest - second * (1.0 / SECOND)) * THIRD).astype(F8)
    zero = jnp.zeros((), jnp.bfloat16)
    span = NODES * SLOT
    masks = [node == jnp.full((), n, jnp.bfloat16) for n in range(NODES)]
    for k, piece in enumerate((first, second, third)):
        piece = piece.astype(jnp.bfloat16)
        rows = jnp.concatenate([jnp.where(mask, piece, zero) for mask in masks], axis=0).astype(F8)
        left_ref[k * span:(k + 1) * span] = rows
        if k == 2:
            left_ref[3 * span:4 * span] = rows


def main_kernel(
    dp, cls, pair, width, parts_ref, nodes_ref, codes_ref, out_ref,
    parts_buf, stats_buf, left_ref, acc_ref, send_buf, recv_buf,
    part_send, part_recv, stat_send, stat_recv, hist_send, hist_recv,
):
    me = lax.axis_index("dp")
    mine = lax.axis_index("cls")
    rows = nodes_ref.shape[1]
    own = codes_ref.shape[1]
    groups = own // pair
    bins = BINS // dp

    def part_copy(e):
        return pltpu.make_async_remote_copy(
            src_ref=parts_buf.at[0], dst_ref=parts_buf.at[e],
            send_sem=part_send.at[e], recv_sem=part_recv.at[e],
            device_id={"cls": lax.rem(mine + e, cls)}, device_id_type=MESH,
        )

    def stat_copy(d):
        return pltpu.make_async_remote_copy(
            src_ref=stats_buf.at[0], dst_ref=stats_buf.at[d],
            send_sem=stat_send.at[d], recv_sem=stat_recv.at[d],
            device_id={"dp": lax.rem(me + d, dp)}, device_id_type=MESH,
        )

    def hist_copy(d):
        to = lax.rem(me + d, dp)
        return pltpu.make_async_remote_copy(
            src_ref=send_buf.at[pl.ds(to * bins, bins)], dst_ref=recv_buf.at[me],
            send_sem=hist_send.at[d], recv_sem=hist_recv.at[d],
            device_id={"dp": to}, device_id_type=MESH,
        )

    barrier = pltpu.get_barrier_semaphore()

    @pl.loop(1, dp)
    def _(d):
        pl.semaphore_signal(barrier, inc=1, device_id={"dp": lax.rem(me + d, dp)}, device_id_type=MESH)

    @pl.loop(1, cls)
    def _(e):
        pl.semaphore_signal(barrier, inc=1, device_id={"cls": lax.rem(mine + e, cls)}, device_id_type=MESH)

    parts_buf[0] = parts_ref[...]
    pl.semaphore_wait(barrier, dp + cls - 2)

    @pl.loop(1, cls)
    def _(e):
        part_copy(e).start()

    acc_ref[...] = jnp.zeros_like(acc_ref)

    @pl.loop(1, cls)
    def _(e):
        part_copy(e).wait_recv()

    stats_buf[0] = combine(parts_buf, nodes_ref)

    @pl.loop(1, dp)
    def _(d):
        stat_copy(d).start()

    bin_ids = lax.broadcasted_iota(jnp.int32, (BINS, width), 0).astype(jnp.bfloat16)
    one = jnp.ones((), jnp.bfloat16)
    zero = jnp.zeros((), jnp.bfloat16)

    @pl.loop(0, dp)
    def _(d):
        @pl.when(d > 0)
        def _():
            stat_copy(d).wait_recv()

        split_weights(stats_buf[d], left_ref)
        source = lax.rem(me - d + dp, dp)
        for f in range(own):
            total = None
            for c in range(rows // width):
                cut = slice(c * width, (c + 1) * width)
                code = codes_ref[source, f:f + 1, cut]
                hit = jnp.where(code == bin_ids, one, zero).astype(F8)
                term = lax.dot_general(hit, left_ref[:, cut], NT, preferred_element_type=jnp.float32)
                total = term if total is None else total + term
            acc_ref[f] += total

    span = NODES * SLOT
    lane = lax.broadcasted_iota(jnp.int32, (BINS, 2 * span), 1)
    scale = jnp.where(lane < span, 1.0 / FIRST, 1.0 / (FIRST * SECOND))

    def whole(f):
        low = acc_ref[f, :, 0:2 * span] * scale
        high = acc_ref[f, :, 2 * span:4 * span] * (1.0 / (FIRST * THIRD))
        return low + pltpu.roll(low, span, 1) + high

    for g in range(groups):
        value = whole(g)
        if pair == 2:
            value = jnp.where(lane < span, value, whole(groups + g))
        send_buf[:, g, :] = value

    @pl.loop(1, dp)
    def _(d):
        hist_copy(d).start()

    recv_buf[me] = send_buf[pl.ds(me * bins, bins)]

    @pl.loop(1, dp)
    def _(d):
        hist_copy(d).wait_recv()

    width_out = dp * groups

    @pl.loop(0, bins)
    def _(b):
        block = recv_buf[:, b].reshape(width_out, 2 * span).T
        for i in range(pair):
            for n in range(NODES):
                at = (i * NODES + n) * SLOT
                out_ref[b, n, :, i * width_out:(i + 1) * width_out] = block[at:at + STATS]

    @pl.loop(1, cls)
    def _(e):
        part_copy(e).wait_send()

    @pl.loop(1, dp)
    def _(d):
        stat_copy(d).wait_send()
        hist_copy(d).wait_send()


def body(dp, cls, scores, labels, node_ids, codes, sketch):
    rows, classes = scores.shape
    feats = codes.shape[1]
    own = feats // dp
    pair = 2 if own % 2 == 0 else 1
    groups = own // pair
    block = min(512, rows)

    codes_t = pl.pallas_call(
        codes_kernel,
        grid=(rows // block,),
        in_specs=[pl.BlockSpec((block, feats), lambda i: (i, 0))],
        out_specs=pl.BlockSpec((feats, block), lambda i: (0, i)),
        out_shape=jax.ShapeDtypeStruct((feats, rows), jnp.bfloat16),
    )(codes)
    codes_t = codes_t.reshape(pair, dp, groups, rows).transpose(1, 0, 2, 3).reshape(dp, own, rows)
    codes_all = lax.all_to_all(codes_t, "dp", 0, 0, tiled=True)

    local = (labels - lax.axis_index("cls") * classes)[None, :]
    left = jnp.concatenate(
        [sketch.T, jnp.ones((1, classes), jnp.float32), jnp.zeros((7, classes), jnp.float32)], axis=0
    )
    parts = pl.pallas_call(
        softmax_kernel,
        grid=(rows // block,),
        in_specs=[
            pl.BlockSpec((block, classes), lambda i: (i, 0)),
            pl.BlockSpec((1, block), lambda i: (0, i)),
            pl.BlockSpec((16, classes), lambda i: (0, 0)),
        ],
        out_specs=pl.BlockSpec((24, block), lambda i: (0, i)),
        out_shape=jax.ShapeDtypeStruct((24, rows), jnp.float32),
    )(scores, local, left)
    bins = BINS // dp
    vmem = pl.BlockSpec(memory_space=pltpu.VMEM)
    return pl.pallas_call(
        functools.partial(main_kernel, dp, cls, pair, min(WIDTH, rows)),
        in_specs=[vmem] * 3,
        out_specs=vmem,
        out_shape=jax.ShapeDtypeStruct((bins, NODES, STATS, feats), jnp.float32),
        scratch_shapes=[
            pltpu.VMEM((cls, 24, rows), jnp.float32),
            pltpu.VMEM((dp, SLOT, rows), jnp.bfloat16),
            pltpu.VMEM((4 * NODES * SLOT, rows), F8),
            pltpu.VMEM((own, BINS, 4 * NODES * SLOT), jnp.float32),
            pltpu.VMEM((BINS, groups, 128), jnp.float32),
            pltpu.VMEM((dp, bins, groups, 128), jnp.float32),
            pltpu.SemaphoreType.DMA((cls,)),
            pltpu.SemaphoreType.DMA((cls,)),
            pltpu.SemaphoreType.DMA((dp,)),
            pltpu.SemaphoreType.DMA((dp,)),
            pltpu.SemaphoreType.DMA((dp,)),
            pltpu.SemaphoreType.DMA((dp,)),
        ],
        compiler_params=pltpu.CompilerParams(
            vmem_limit_bytes=50 << 20, collective_id=0, has_side_effects=True
        ),
    )(parts, node_ids[None, :], codes_all)


WIDTH = 512


def solution(mesh):
    return jax.shard_map(
        functools.partial(body, mesh.shape["dp"], mesh.shape["cls"]),
        mesh=mesh,
        in_specs=(P("dp", "cls"), P("dp"), P("dp"), P("dp", "cls"), P("cls", None)),
        out_specs=P("dp", None, None, "cls"),
        check_vma=False,
    )
```

```python
import functools

import jax
import jax.numpy as jnp
from jax import lax
from jax.experimental import pallas as pl
from jax.experimental.pallas import tpu as pltpu
from jax.sharding import PartitionSpec as P

BINS = 256
NODES = 4
STATS = 9
SLOT = 16
MESH = pl.DeviceIdType.MESH
F8 = jnp.float8_e4m3fn
FIRST, SECOND, THIRD = 32.0, 16.0, float(2**22)
NT = (((1,), (1,)), ((), ()))


def turn_codes(codes_ref, codes_send, pair, block):
    rows, feats = codes_ref.shape
    dp, own, _ = codes_send.shape
    groups = own // pair

    @pl.loop(0, rows // block)
    def _(i):
        at = pl.ds(pl.multiple_of(i * block, block), block)
        turned = codes_ref[at].astype(jnp.float32).T
        for k in range(dp):
            picked = [turned[(j * dp + k) * groups:(j * dp + k + 1) * groups] for j in range(pair)]
            picked = picked[0] if pair == 1 else jnp.concatenate(picked, axis=0)
            codes_send[k, :, at] = picked.astype(jnp.bfloat16)


def class_sums(scores_ref, labels_ref, sketch_ref, parts_buf, first_class, block):
    rows, classes = scores_ref.shape
    sketch = sketch_ref[...]
    high = sketch.astype(jnp.bfloat16)
    rest = sketch - high.astype(jnp.float32)
    mid = rest.astype(jnp.bfloat16)
    low = rest - mid.astype(jnp.float32)
    left = jnp.concatenate(
        [high.astype(jnp.float32), mid.astype(jnp.float32), low, jnp.zeros_like(low)], axis=0
    ).astype(jnp.bfloat16)
    one = jnp.ones((), jnp.float32)
    zero = jnp.zeros((), jnp.float32)
    class_ids = lax.broadcasted_iota(jnp.int32, (classes, block), 0)
    where = lax.broadcasted_iota(jnp.int32, (8, block), 0)

    def times(right):
        out = jnp.dot(left, right, preferred_element_type=jnp.float32)
        return out[0:8] + out[8:16] + out[16:24]

    @pl.loop(0, rows // block)
    def _(i):
        at = pl.ds(pl.multiple_of(i * block, block), block)
        values = scores_ref[at].astype(jnp.float32).T
        top = jnp.max(values, axis=0, keepdims=True)
        expo = jnp.exp(values - top)
        total = jnp.sum(expo, axis=0, keepdims=True)
        squares = jnp.sum(expo * expo, axis=0, keepdims=True)
        coarse = expo.astype(jnp.bfloat16)
        fine = (expo - coarse.astype(jnp.float32)).astype(jnp.bfloat16)
        hit = jnp.where(class_ids == labels_ref[:, at] - first_class, one, zero).astype(jnp.bfloat16)
        parts_buf[0, 0:8, at] = times(coarse) + times(fine)
        parts_buf[0, 8:16, at] = times(hit)
        parts_buf[0, 16:24, at] = jnp.where(where == 0, top, jnp.where(where == 1, total, squares))


def combine(parts_ref, nodes_ref):
    parts = parts_ref.shape[0]
    top = parts_ref[0, 16:17]
    for i in range(1, parts):
        top = jnp.maximum(top, parts_ref[i, 16:17])
    sketched = label = total = squares = 0.0
    for i in range(parts):
        scale = jnp.exp(parts_ref[i, 16:17] - top)
        sketched += parts_ref[i, 0:8] * scale
        label += parts_ref[i, 8:16]
        total += parts_ref[i, 17:18] * scale
        squares += parts_ref[i, 18:19] * (scale * scale)
    grad = sketched / total - label
    hessian = 1.0 - squares / (total * total)
    where = lax.broadcasted_iota(jnp.int32, grad.shape, 0)
    tail = jnp.where(where == 0, hessian, jnp.where(where == 1, nodes_ref[...].astype(jnp.float32), 0.0))
    return jnp.concatenate([grad, tail], axis=0).astype(jnp.bfloat16)


def split_weights(stats, left_ref):
    node = stats[STATS:STATS + 1]
    wide = stats.astype(jnp.float32) * FIRST
    wide = jnp.where(lax.broadcasted_iota(jnp.int32, wide.shape, 0) < STATS, wide, 0.0)
    first = wide.astype(F8).astype(jnp.float32)
    rest = wide - first
    second = (rest * SECOND).astype(F8).astype(jnp.float32)
    third = ((rest - second * (1.0 / SECOND)) * THIRD).astype(F8)
    zero = jnp.zeros((), jnp.bfloat16)
    span = NODES * SLOT
    masks = [node == jnp.full((), n, jnp.bfloat16) for n in range(NODES)]
    for k, piece in enumerate((first, second, third)):
        piece = piece.astype(jnp.bfloat16)
        rows = jnp.concatenate([jnp.where(mask, piece, zero) for mask in masks], axis=0).astype(F8)
        left_ref[k * span:(k + 1) * span] = rows
        if k == 2:
            left_ref[3 * span:4 * span] = rows


def main_kernel(
    dp, cls, pair, width, scores_ref, labels_ref, nodes_ref, codes_ref, sketch_ref, out_ref,
    codes_send, codes_buf, parts_buf, stats_buf, left_ref, acc_ref, send_buf, recv_buf,
    code_send, code_recv, part_send, part_recv, stat_send, stat_recv, hist_send, hist_recv,
):
    me = lax.axis_index("dp")
    mine = lax.axis_index("cls")
    rows = nodes_ref.shape[1]
    own = codes_buf.shape[1]
    groups = own // pair
    bins = BINS // dp

    def code_copy(d):
        to = lax.rem(me + d, dp)
        return pltpu.make_async_remote_copy(
            src_ref=codes_send.at[to], dst_ref=codes_buf.at[d],
            send_sem=code_send.at[d], recv_sem=code_recv.at[d],
            device_id={"dp": to}, device_id_type=MESH,
        )

    def part_copy(e):
        return pltpu.make_async_remote_copy(
            src_ref=parts_buf.at[0], dst_ref=parts_buf.at[e],
            send_sem=part_send.at[e], recv_sem=part_recv.at[e],
            device_id={"cls": lax.rem(mine + e, cls)}, device_id_type=MESH,
        )

    def stat_copy(d):
        return pltpu.make_async_remote_copy(
            src_ref=stats_buf.at[0], dst_ref=stats_buf.at[d],
            send_sem=stat_send.at[d], recv_sem=stat_recv.at[d],
            device_id={"dp": lax.rem(me + d, dp)}, device_id_type=MESH,
        )

    def hist_copy(d):
        to = lax.rem(me + d, dp)
        return pltpu.make_async_remote_copy(
            src_ref=send_buf.at[pl.ds(to * bins, bins)], dst_ref=recv_buf.at[me],
            send_sem=hist_send.at[d], recv_sem=hist_recv.at[d],
            device_id={"dp": to}, device_id_type=MESH,
        )

    barrier = pltpu.get_barrier_semaphore()

    @pl.loop(1, dp)
    def _(d):
        pl.semaphore_signal(barrier, inc=1, device_id={"dp": lax.rem(me + d, dp)}, device_id_type=MESH)

    @pl.loop(1, cls)
    def _(e):
        pl.semaphore_signal(barrier, inc=1, device_id={"cls": lax.rem(mine + e, cls)}, device_id_type=MESH)

    turn_codes(codes_ref, codes_send, pair, min(BLOCK, rows))
    pl.semaphore_wait(barrier, dp + cls - 2)

    @pl.loop(1, dp)
    def _(d):
        code_copy(d).start()

    codes_buf[0] = codes_send[me]
    class_sums(
        scores_ref, labels_ref, sketch_ref, parts_buf, mine * scores_ref.shape[1], min(BLOCK, rows)
    )

    @pl.loop(1, cls)
    def _(e):
        part_copy(e).start()

    acc_ref[...] = jnp.zeros_like(acc_ref)

    @pl.loop(1, cls)
    def _(e):
        part_copy(e).wait_recv()

    stats_buf[0] = combine(parts_buf, nodes_ref)

    @pl.loop(1, dp)
    def _(d):
        stat_copy(d).start()

    bin_ids = lax.broadcasted_iota(jnp.int32, (BINS, width), 0).astype(jnp.bfloat16)
    one = jnp.ones((), jnp.bfloat16)
    zero = jnp.zeros((), jnp.bfloat16)

    @pl.loop(0, dp)
    def _(d):
        @pl.when(d > 0)
        def _():
            code_copy(d).wait_recv()
            stat_copy(d).wait_recv()

        split_weights(stats_buf[d], left_ref)
        for f in range(own):
            total = None
            for c in range(rows // width):
                cut = slice(c * width, (c + 1) * width)
                code = codes_buf[d, f:f + 1, cut]
                hit = jnp.where(code == bin_ids, one, zero).astype(F8)
                term = lax.dot_general(hit, left_ref[:, cut], NT, preferred_element_type=jnp.float32)
                total = term if total is None else total + term
            acc_ref[f] += total

    span = NODES * SLOT
    lane = lax.broadcasted_iota(jnp.int32, (BINS, 2 * span), 1)
    scale = jnp.where(lane < span, 1.0 / FIRST, 1.0 / (FIRST * SECOND))

    def whole(f):
        low = acc_ref[f, :, 0:2 * span] * scale
        high = acc_ref[f, :, 2 * span:4 * span] * (1.0 / (FIRST * THIRD))
        return low + pltpu.roll(low, span, 1) + high

    for g in range(groups):
        value = whole(g)
        if pair == 2:
            value = jnp.where(lane < span, value, whole(groups + g))
        send_buf[:, g, :] = value

    @pl.loop(1, dp)
    def _(d):
        hist_copy(d).start()

    recv_buf[me] = send_buf[pl.ds(me * bins, bins)]

    @pl.loop(1, dp)
    def _(d):
        hist_copy(d).wait_recv()

    width_out = dp * groups

    @pl.loop(0, bins)
    def _(b):
        block = recv_buf[:, b].reshape(width_out, 2 * span).T
        for i in range(pair):
            for n in range(NODES):
                at = (i * NODES + n) * SLOT
                out_ref[b, n, :, i * width_out:(i + 1) * width_out] = block[at:at + STATS]

    @pl.loop(1, cls)
    def _(e):
        part_copy(e).wait_send()

    @pl.loop(1, dp)
    def _(d):
        code_copy(d).wait_send()
        stat_copy(d).wait_send()
        hist_copy(d).wait_send()


def body(dp, cls, scores, labels, node_ids, codes, sketch):
    rows = scores.shape[0]
    feats = codes.shape[1]
    own = feats // dp
    pair = 2 if own % 2 == 0 else 1
    groups = own // pair
    bins = BINS // dp
    vmem = pl.BlockSpec(memory_space=pltpu.VMEM)
    return pl.pallas_call(
        functools.partial(main_kernel, dp, cls, pair, min(WIDTH, rows)),
        in_specs=[vmem] * 5,
        out_specs=vmem,
        out_shape=jax.ShapeDtypeStruct((bins, NODES, STATS, feats), jnp.float32),
        scratch_shapes=[
            pltpu.VMEM((dp, own, rows), jnp.bfloat16),
            pltpu.VMEM((dp, own, rows), jnp.bfloat16),
            pltpu.VMEM((cls, 24, rows), jnp.float32),
            pltpu.VMEM((dp, SLOT, rows), jnp.bfloat16),
            pltpu.VMEM((4 * NODES * SLOT, rows), F8),
            pltpu.VMEM((own, BINS, 4 * NODES * SLOT), jnp.float32),
            pltpu.VMEM((BINS, groups, 128), jnp.float32),
            pltpu.VMEM((dp, bins, groups, 128), jnp.float32),
            pltpu.SemaphoreType.DMA((dp,)),
            pltpu.SemaphoreType.DMA((dp,)),
            pltpu.SemaphoreType.DMA((cls,)),
            pltpu.SemaphoreType.DMA((cls,)),
            pltpu.SemaphoreType.DMA((dp,)),
            pltpu.SemaphoreType.DMA((dp,)),
            pltpu.SemaphoreType.DMA((dp,)),
            pltpu.SemaphoreType.DMA((dp,)),
        ],
        compiler_params=pltpu.CompilerParams(
            vmem_limit_bytes=50 << 20, collective_id=0, has_side_effects=True
        ),
    )(scores, labels[None, :], node_ids[None, :], codes, sketch.T)


WIDTH = 512
BLOCK = 256


def solution(mesh):
    return jax.shard_map(
        functools.partial(body, mesh.shape["dp"], mesh.shape["cls"]),
        mesh=mesh,
        in_specs=(P("dp", "cls"), P("dp"), P("dp"), P("dp", "cls"), P("cls", None)),
        out_specs=P("dp", None, None, "cls"),
        check_vma=False,
    )
```
